32 devices in a mesh: section: 2 (over core), mesh: 16 (over z, y, x).
Axes of the slice: x: 2, y: 2, z: 4, core: 2. Of those that a mesh axis runs over, the one named last changes fastest.
Arguments:
- saved_inputs: bfloat16 [2, 3, 4096, 1024], P('section', None, 'mesh'), may hold values from -8 to 8
- w_query: bfloat16 [2, 1024, 1024], P('section'), may hold values from -6 to 6
- w_key: bfloat16 [2, 1024, 1024], P('section'), may hold values from -6 to 6
- w_value: bfloat16 [2, 1024, 1024], P('section'), may hold values from -0.1875 to 0.1875
- w_out: bfloat16 [2, 1024, 1024], P('section'), may hold values from -0.1875 to 0.1875
- pending: bfloat16 [2, 4096, 1024], P('section', 'mesh'), may hold values from -6 to 6
- top_grads: bfloat16 [1, 4096, 1024], P(None, 'mesh'), may hold values from -6 to 6
- key_blocks: int32 [32, 2], P('mesh'), may hold values from -1 to 31, as said below
- counts: int32 [32], replicated, may hold values from 64 to 128, as said below
- plan: int32 [2, 2], replicated, may hold values from 0 to 2
Outputs:
- layer_grads: float32 [2, 1024, 4, 1024], P('section', 'mesh')
- input_grads: bfloat16 [2, 2, 4096, 1024], P(None, 'section', 'mesh')
The draws below stay inside these ranges and needn't reach their ends.
Inputs may be any that keep to these rules, and one draw needn't show every extreme that they name: `key_blocks`: entry j of block b is -1 (nothing read) or the block (b + o_j) modulo 32, with o = (1, -1). `counts`: the padding nodes of a block are its last ones.
All inputs are finite; a program needn't handle non-finite values.
Results may differ from the reference program's by a relative error of at most 0.03.
The reference program's roundings to bfloat16 on the way count: a program that leaves them out, or rounds other values in their place, can miss the bound.
Values may be sent and summed in bfloat16 or wider, within the bound.
A program may use at most 128 MiB of HBM per device.

```python
import math
import jax
import jax.numpy as jnp
import numpy as np
from jax import lax

D = 1024
HEADS = 8
HEAD_DIM = 128
BLOCK = 128
BLOCKS_DEV = 2
MEMBERS = 3
TICKS = 2
SECTIONS = 2
NODES = 4096


OFFSET_TABLE = (1, -1)


def draw_saved_inputs(key, part):
    full_shape = (SECTIONS, MEMBERS, NODES, D)
    normal_draw = jax.random.normal(jax.random.fold_in(key, 1), full_shape, jnp.float32)
    return jnp.clip(normal_draw, -6.0, 6.0).astype(jnp.bfloat16)


def projection_draw(key, salt):
    base = jax.random.normal(jax.random.fold_in(key, salt), (SECTIONS, D, D), jnp.float32) / math.sqrt(D)
    base = jnp.clip(base, -6.0 / math.sqrt(D), 6.0 / math.sqrt(D))
    return base


def draw_w_query(key, part):
    return projection_draw(key, 11).astype(jnp.bfloat16)


def draw_w_key(key, part):
    return projection_draw(key, 23).astype(jnp.bfloat16)


def draw_key_blocks(key, part):
    block_count = NODES // BLOCK
    offsets = jnp.array(OFFSET_TABLE, jnp.int32)
    owners = (jnp.arange(block_count, dtype=jnp.int32)[:, None] + offsets[None, :]) % block_count
    dice_rolls = jax.random.randint(jax.random.fold_in(key, 5), (block_count, 2), 0, 5)
    row_index = jnp.arange(block_count)[:, None]
    col_index = jnp.arange(2)[None, :]
    is_live = (dice_rolls < 3) | (row_index == 0)
    is_live = is_live & jnp.logical_not((row_index == 1) & (col_index == 0))
    return jnp.where(is_live, owners, -1).astype(jnp.int32)


def draw_counts(key, part):
    block_count = NODES // BLOCK
    drawn = jax.random.randint(jax.random.fold_in(key, 7), (block_count,), BLOCK // 2, BLOCK + 1)
    index_list = jnp.arange(block_count)
    drawn = jnp.where(index_list == 0, BLOCK, drawn)
    drawn = jnp.where(index_list == 1, BLOCK // 2, drawn)
    return drawn.astype(jnp.int32)


def place_ends(result, key, smallest, largest):
    longest = result.shape.index(max(result.shape))
    spots = []
    for shift in (0, 1):
        where = [jax.random.randint(jax.random.fold_in(key, axis), (), 0, length) for axis, length in enumerate(result.shape)]
        where[longest] = (where[longest] + shift) % result.shape[longest]
        spots.append(tuple(where))
    return result.at[spots[0]].set(smallest).at[spots[1]].set(largest)


def level_of(key, extent, cuts, low, top_value):
    def one(dim, shards_of):
        draws = jax.random.uniform(jax.random.fold_in(jax.random.fold_in(key, 6), dim), (shards_of,), jnp.float32, low / len(cuts), top_value / len(cuts))
        return jnp.repeat(jnp.exp(draws), extent[dim] // shards_of).reshape((-1,) + (1,) * (len(extent) - dim - 1))

    gain = one(*cuts[0])
    for cut in cuts[1:]:
        gain = gain * one(*cut)
    return gain


def gaussian(own_key, shape, deviation, bound, split=(), kind=jnp.bfloat16):
    values = jax.random.normal(own_key, shape, jnp.float32) * deviation
    if len(split) > 0:
        values = level_of(own_key, shape, split, -0.22, 0.18) * values
    return jnp.clip(values, min=-bound, max=bound).astype(kind)


def setup_inputs(seed: int = 0) -> dict:
    splits = jax.random.split(jax.random.key(seed), 11)
    return {
        "saved_inputs": draw_saved_inputs(jax.random.fold_in(splits[10], 71), 0),
        "w_query": draw_w_query(jax.random.fold_in(splits[10], 71), 0),
        "w_key": draw_w_key(jax.random.fold_in(splits[10], 71), 0),
        "w_value": gaussian(splits[3], (SECTIONS, D, D), D ** -0.5, 0.1875, ((0, 2),)),
        "w_out": gaussian(splits[4], (SECTIONS, D, D), D ** -0.5, 0.1875, ((0, 2),)),
        "pending": gaussian(splits[5], (SECTIONS, NODES, D), 1.0, 6.0, ((0, 2), (1, 16))),
        "top_grads": gaussian(splits[6], (TICKS - 1, NODES, D), 1.0, 6.0, ((1, 16),)),
        "key_blocks": draw_key_blocks(jax.random.fold_in(splits[10], 71), 0),
        "counts": draw_counts(jax.random.fold_in(splits[10], 71), 0),
        "plan": place_ends(jax.random.randint(splits[9], (TICKS, SECTIONS), 0, MEMBERS), jax.random.fold_in(splits[9], 1), 0, MEMBERS - 1).astype(jnp.int32),
    }


OFFSETS = (1, -1)
EPSILON = 1e-06

def right_dot(left, right):
    return lax.dot_general(left, right, (((1,), (1,)), ((), ())), preferred_element_type=jnp.float32)

def left_dot(left, right):
    return lax.dot_general(left, right, (((0,), (0,)), ((), ())), preferred_element_type=jnp.float32)

def round_trip(values):
    return lax.optimization_barrier(values.astype(jnp.bfloat16)).astype(jnp.float32)

def key_mask(key_blocks, counts):
    positions = jnp.arange(BLOCK)
    pieces = [positions[None, :] < counts[:, None]]
    for slot_index in range(len(OFFSETS)):
        listed = key_blocks[:, slot_index]
        remote_count = jnp.where(listed >= 0, counts[jnp.maximum(listed, 0)], 0)
        pieces.append(positions[None, :] < remote_count[:, None])
    return jnp.concatenate(pieces, axis=1)

def layer_back(x_in, query_weight, key_weight, value_weight, out_weight, upstream, mask):
    block_count = NODES // BLOCK
    part_count = block_count // BLOCKS_DEV
    slot_count = 1 + len(OFFSETS)
    score_scale = 1.0 / math.sqrt(HEAD_DIM)
    x_float = x_in.astype(jnp.float32)
    inv_rms = lax.rsqrt(lax.optimization_barrier(jnp.mean(x_float * x_float, axis=-1, keepdims=True)) + EPSILON)
    normed_float = x_float * inv_rms
    normed = normed_float.astype(jnp.bfloat16)
    queries = jnp.dot(normed, query_weight, preferred_element_type=jnp.float32).astype(jnp.bfloat16)
    key_rows = jnp.dot(normed, key_weight, preferred_element_type=jnp.float32).astype(jnp.bfloat16)
    value_rows = jnp.dot(normed, value_weight, preferred_element_type=jnp.float32).astype(jnp.bfloat16)

    def spread(rows):
        blocks = rows.reshape(block_count, BLOCK, D)
        listed = [blocks] + [jnp.roll(blocks, -offset, axis=0) for offset in OFFSETS]
        joined = jnp.concatenate(listed, axis=1)
        return joined.reshape(block_count, slot_count * BLOCK, HEADS, HEAD_DIM).astype(jnp.float32)
    keys_all = spread(key_rows)
    values_all = spread(value_rows)
    query_heads = queries.reshape(block_count, BLOCK, HEADS, HEAD_DIM).astype(jnp.float32)
    scores = jnp.einsum('pqhd,pkhd->phqk', query_heads, keys_all) * score_scale
    scores = jnp.where(mask[:, None, None, :], scores, -jnp.inf)
    peak = lax.optimization_barrier(jnp.max(scores, axis=-1, keepdims=True))
    raised = jnp.exp(scores - peak)
    probs = raised / lax.optimization_barrier(jnp.sum(raised, axis=-1, keepdims=True))
    probs_round = round_trip(probs)
    attended = jnp.einsum('phqk,pkhd->pqhd', probs_round, values_all).reshape(NODES, D).astype(jnp.bfloat16)
    grad_attended = right_dot(upstream, out_weight).astype(jnp.bfloat16)
    grad_heads = grad_attended.reshape(block_count, BLOCK, HEADS, HEAD_DIM).astype(jnp.float32)
    grad_probs = jnp.einsum('pqhd,pkhd->phqk', grad_heads, values_all)
    grad_scores = probs * (grad_probs - lax.optimization_barrier(jnp.sum(probs * grad_probs, axis=-1, keepdims=True))) * score_scale
    scores_round = round_trip(grad_scores)
    grad_query = jnp.einsum('phqk,pkhd->pqhd', scores_round, keys_all).reshape(NODES, D).astype(jnp.bfloat16)
    key_terms = jnp.einsum('phqk,pqhd->pkhd', scores_round, query_heads).reshape(block_count, slot_count, BLOCK, D)
    value_terms = jnp.einsum('phqk,pqhd->pkhd', probs_round, grad_heads).reshape(block_count, slot_count, BLOCK, D)
    block_owner = np.arange(block_count) // BLOCKS_DEV
    pair_terms = jnp.stack([key_terms, value_terms])
    local_sum = pair_terms[:, :, 0]
    from_before = jnp.zeros_like(local_sum)
    from_after = jnp.zeros_like(local_sum)
    for slot_index, offset in enumerate(OFFSETS):
        moved = jnp.roll(pair_terms[:, :, 1 + slot_index], offset, axis=1)
        source_owner = np.roll(block_owner, offset)
        delta = (source_owner - block_owner) % part_count
        same_mask = jnp.asarray(delta == 0)[None, :, None, None]
        before_mask = jnp.asarray(delta == part_count - 1)[None, :, None, None]
        after_mask = jnp.asarray(delta == 1)[None, :, None, None]
        local_sum = local_sum + jnp.where(same_mask, moved, 0.0)
        from_before = from_before + jnp.where(before_mask, moved, 0.0)
        from_after = from_after + jnp.where(after_mask, moved, 0.0)
    pair_total = local_sum + round_trip(from_before) + round_trip(from_after)
    grad_key = pair_total[0].reshape(NODES, D).astype(jnp.bfloat16)
    grad_value = pair_total[1].reshape(NODES, D).astype(jnp.bfloat16)
    grad_normed = right_dot(grad_query, query_weight) + right_dot(grad_key, key_weight) + right_dot(grad_value, value_weight)
    grad_input = inv_rms * (grad_normed - normed_float * lax.optimization_barrier(jnp.mean(grad_normed * normed_float, axis=-1, keepdims=True)))
    grad_x = (upstream.astype(jnp.float32) + grad_input).astype(jnp.bfloat16)
    return (grad_x, (normed, grad_query, grad_key, grad_value, attended, upstream))

def section_weights(stored):
    part_rows = BLOCKS_DEV * BLOCK
    part_count = NODES // part_rows

    def one_part(total, part_index):
        first_row = part_index * part_rows
        for terms in stored:
            rows = [lax.dynamic_slice_in_dim(array, first_row, part_rows, 0) for array in terms]
            normed, grad_query, grad_key, grad_value, attended, upstream = rows
            stacked = jnp.stack([left_dot(normed, grad_query), left_dot(normed, grad_key), left_dot(normed, grad_value), left_dot(attended, upstream)], axis=1)
            total = total + round_trip(stacked)
        return (total, None)
    return lax.scan(one_part, jnp.zeros((D, 4, D), jnp.float32), jnp.arange(part_count, dtype=jnp.int32))[0]

def reference(saved_inputs, w_query, w_key, w_value, w_out, pending, top_grads, key_blocks, counts, plan):
    mask = key_mask(key_blocks, counts)
    grads_by_section = [None] * SECTIONS
    inputs_by_section = [None] * SECTIONS
    from_above = None
    for section_index in range(SECTIONS - 1, -1, -1):
        outgoing = []
        stored = []
        for tick_index in range(TICKS):
            if tick_index == 0:
                upstream = pending[section_index]
            elif section_index == SECTIONS - 1:
                upstream = top_grads[tick_index - 1]
            else:
                upstream = from_above[tick_index - 1]
            member = plan[tick_index, section_index]
            x_in = lax.dynamic_index_in_dim(saved_inputs[section_index], member, 0, keepdims=False)
            grad_x, terms = layer_back(x_in, w_query[section_index], w_key[section_index], w_value[section_index], w_out[section_index], upstream, mask)
            outgoing.append(grad_x)
            stored.append(terms)
        grads_by_section[section_index] = section_weights(stored)
        inputs_by_section[section_index] = jnp.stack(outgoing)
        from_above = outgoing
    return (jnp.stack(grads_by_section), jnp.stack(inputs_by_section, axis=1))
```

```python
import functools
import math

import jax
import jax.numpy as jnp
from jax import lax
from jax.experimental import pallas as pl
from jax.experimental.pallas import tpu as pltpu
from jax.sharding import PartitionSpec as P

HEADS = 8
BLOCK = 128
OFFSETS = (1, -1)
EPSILON = 1e-06
MESH = pl.DeviceIdType.MESH


def from_behind(value, axis, steps):
    count = lax.axis_size(axis)
    pairs = [(source, (source + steps) % count) for source in range(count)]
    return lax.ppermute(value, axis, pairs)


def shifted(x, axis, by):
    size = lax.axis_size(axis)
    pairs = [(i, i + by) for i in range(size) if 0 <= i + by < size]
    return lax.ppermute(x, axis, pairs)


def right_dot(left, right):
    return lax.dot_general(
        left, right, (((1,), (1,)), ((), ())), preferred_element_type=jnp.float32
    )


def left_dot(left, right):
    return lax.dot_general(
        left, right, (((0,), (0,)), ((), ())), preferred_element_type=jnp.float32
    )


def plain_dot(left, right):
    return jnp.dot(left, right, preferred_element_type=jnp.float32)


def attention_kernel(
    scale, q_ref, ko_ref, vo_ref, kh_ref, vh_ref, ga_ref, mask_ref,
    att_ref, gq_ref, kto_ref, vto_ref, kth_ref, vth_ref,
):
    size = BLOCK
    keys = jnp.concatenate([kh_ref[:size], ko_ref[...], kh_ref[size:]], axis=0)
    values = jnp.concatenate([vh_ref[:size], vo_ref[...], vh_ref[size:]], axis=0)
    blocks = q_ref.shape[0] // size
    key_sums = [None] * (blocks + 2)
    value_sums = [None] * (blocks + 2)
    for b in range(blocks):
        rows = slice(b * size, (b + 1) * size)
        near = slice(b * size, (b + 3) * size)
        q = q_ref[rows]
        ga = ga_ref[rows]
        k = keys[near]
        v = values[near]
        scores = right_dot(q, k) * scale + mask_ref[b : b + 1, :]
        raised = jnp.exp(scores - jnp.max(scores, axis=-1, keepdims=True))
        probs = raised / jnp.sum(raised, axis=-1, keepdims=True)
        probs_bf = probs.astype(jnp.bfloat16)
        att_ref[:, rows] = lax.dot_general(
            v, probs_bf, (((0,), (1,)), ((), ())), preferred_element_type=jnp.float32
        ).astype(jnp.bfloat16)
        grad_probs = right_dot(ga, v)
        inner = jnp.sum(probs * grad_probs, axis=-1, keepdims=True)
        scores_bf = (probs * (grad_probs - inner) * scale).astype(jnp.bfloat16)
        gq_ref[rows] = plain_dot(scores_bf, k).astype(jnp.bfloat16)
        key_terms = left_dot(scores_bf, q)
        value_terms = left_dot(probs_bf, ga)
        for j in range(3):
            part = slice(j * size, (j + 1) * size)
            for sums, terms in ((key_sums, key_terms), (value_sums, value_terms)):
                old = sums[b + j]
                sums[b + j] = terms[part] if old is None else old + terms[part]
    for sums, own, halo in ((key_sums, kto_ref, kth_ref), (value_sums, vto_ref, vth_ref)):
        halo[:size] = sums[0].astype(jnp.bfloat16)
        halo[size:] = sums[blocks + 1].astype(jnp.bfloat16)
        for b in range(blocks):
            own[b * size : (b + 1) * size] = sums[b + 1].astype(jnp.bfloat16)


def attention(tick, q, ko, vo, kh, vh, ga, mask):
    rows, features = q.shape[1:]
    dim = features // HEADS
    halo = kh.shape[1]
    ticked = lambda n: pl.BlockSpec((None, n, dim), lambda h: (tick, 0, h))
    flat = lambda n: pl.BlockSpec((n, dim), lambda h: (0, h))
    shape = lambda n: jax.ShapeDtypeStruct((n, features), jnp.bfloat16)
    return pl.pallas_call(
        functools.partial(attention_kernel, 1.0 / math.sqrt(dim)),
        grid=(HEADS,),
        in_specs=[
            ticked(rows), ticked(rows), ticked(rows), ticked(halo), ticked(halo), flat(rows),
            pl.BlockSpec(mask.shape, lambda h: (0, 0)),
        ],
        out_specs=[
            pl.BlockSpec((dim, rows), lambda h: (h, 0)),
            flat(rows), flat(rows), flat(rows), flat(halo), flat(halo),
        ],
        out_shape=[
            jax.ShapeDtypeStruct((features, rows), jnp.bfloat16),
            shape(rows), shape(rows), shape(rows), shape(halo), shape(halo),
        ],
        cost_estimate=pl.CostEstimate(
            flops=12 * rows * 3 * BLOCK * features,
            bytes_accessed=24 * rows * features,
            transcendentals=rows * 3 * BLOCK * HEADS,
        ),
        name="attention_both_ways",
    )(q, ko, vo, kh, vh, ga, mask)


def bit_orders(bits):
    swapped = [1, 0] + list(range(2, bits))
    late = list(range(2, bits)) + [0, 1]
    return (list(range(bits)), swapped, late)


PORTIONS = (
    (0, 0, 0), (0, 1, 1), (3, 1, 2), (1, 0, 0), (1, 1, 1), (2, 0, 0), (2, 1, 1), (3, 0, 0),
)


def weight_kernel(
    count, nown_ref, nhalo_ref, att0_ref, att1_ref, gq0, gq1, up0, up1,
    ko0, ko1, kh0, kh1, vo0, vo1, vh0, vh1,
    out_ref, nlhs, alhs, keep, send, recv, send_sem, recv_sem,
):
    me = lax.axis_index("mesh")
    bits = count.bit_length() - 1
    orders = bit_orders(bits)
    features = nown_ref.shape[0]
    chunk = features // count
    half_columns = features // 2

    def bit_of(b):
        return lax.rem(me // (1 << b), 2)

    def partner(b):
        return me + (1 - 2 * bit_of(b)) * (1 << b)

    barrier = pltpu.get_barrier_semaphore()
    for b in range(bits):
        pl.semaphore_signal(barrier, inc=1, device_id={"mesh": partner(b)}, device_id_type=MESH)
    pl.semaphore_wait(barrier, bits)

    own = nown_ref.shape[1]
    halo = nhalo_ref.shape[1]
    tick = att0_ref.shape[1]

    def chunk_rows(order, place):
        index = 0
        for k, b in enumerate(order):
            here = bit_of(b)
            flip = (place >> (bits - 1 - k)) & 1
            index = index + (1 - here if flip else here) * (1 << b)
        return pl.ds(pl.multiple_of(index * chunk, chunk), chunk)

    def arrange(places):
        for place in places:
            to = slice(place * chunk, (place + 1) * chunk)
            for slot in (0, 1):
                rows = chunk_rows(orders[slot], place)
                nlhs[slot, to, :own] = nown_ref[rows, :]
                nlhs[slot, to, own:] = nhalo_ref[rows, :]
                rows = chunk_rows(orders[2 * slot], place)
                alhs[slot, to, :tick] = att0_ref[rows, :]
                alhs[slot, to, tick:] = att1_ref[rows, :]

    rights = ((gq0, gq1), (ko0, ko1, kh0, kh1), (vo0, vo1, vh0, vh1), (up0, up1))

    def product(portion, rows):
        projection, side, order = portion
        columns = slice(side * half_columns, (side + 1) * half_columns)
        right = jnp.concatenate([r[:, columns] for r in rights[projection]], axis=0)
        if projection == 3:
            left = alhs[0 if order == 0 else 1, rows, :]
        else:
            left = nlhs[order, rows, : right.shape[0]]
        return plain_dot(left, right)

    starts = []
    first = 0
    for k in range(bits):
        starts.append(first)
        first += features >> (k + 1)

    def copy_of(p, k):
        rows = pl.ds(starts[k], features >> (k + 1))
        return pltpu.make_async_remote_copy(
            src_ref=send.at[p, rows],
            dst_ref=recv.at[p, rows],
            send_sem=send_sem.at[p, k],
            recv_sem=recv_sem.at[p, k],
            device_id={"mesh": partner(orders[PORTIONS[p][2]][k])},
            device_id_type=MESH,
        )

    middle = features // 2
    arrange(range(count // 2, count))
    for p, portion in enumerate(PORTIONS):
        send[p, :middle] = product(portion, slice(middle, features)).astype(jnp.bfloat16)
        copy_of(p, 0).start()
    arrange(range(count // 2))
    for p, portion in enumerate(PORTIONS):
        keep[p] = product(portion, slice(0, middle))
    for k in range(bits):
        size = features >> (k + 1)
        for p, (projection, side, _) in enumerate(PORTIONS):
            copy_of(p, k).wait_recv()
            if k + 1 < bits:
                left = size // 2
                send[p, starts[k + 1] : starts[k + 1] + left] = (
                    keep[p, left:size]
                    + recv[p, starts[k] + left : starts[k] + size].astype(jnp.float32)
                ).astype(jnp.bfloat16)
                copy_of(p, k + 1).start()
                keep[p, :left] += recv[p, starts[k] : starts[k] + left].astype(jnp.float32)
            else:
                columns = slice(side * half_columns, (side + 1) * half_columns)
                out_ref[projection, :, columns] = keep[p, :size] + recv[
                    p, starts[k] : starts[k] + size
                ].astype(jnp.float32)
    for k in range(bits):
        for p in range(len(PORTIONS)):
            copy_of(p, k).wait_send()


def weight_sums(normed_own, normed_halo, att, gq, up, ko, kh, vo, vh):
    count = lax.axis_size("mesh")
    bits = count.bit_length() - 1
    features = normed_own.shape[0]
    own = normed_own.shape[1]
    halo = normed_halo.shape[1]
    chunk = features // count
    portions = len(PORTIONS)
    moved = features - chunk
    half_columns = features // 2
    return pl.pallas_call(
        functools.partial(weight_kernel, count),
        out_shape=jax.ShapeDtypeStruct((4, chunk, features), jnp.float32),
        in_specs=[pl.BlockSpec(memory_space=pltpu.VMEM)] * 16,
        out_specs=pl.BlockSpec(memory_space=pltpu.VMEM),
        scratch_shapes=[
            pltpu.VMEM((2, features, own + halo), jnp.bfloat16),
            pltpu.VMEM((2, features, own), jnp.bfloat16),
            pltpu.VMEM((portions, features // 2, half_columns), jnp.float32),
            pltpu.VMEM((portions, moved, half_columns), jnp.bfloat16),
            pltpu.VMEM((portions, moved, half_columns), jnp.bfloat16),
            pltpu.SemaphoreType.DMA((portions, bits)),
            pltpu.SemaphoreType.DMA((portions, bits)),
        ],
        compiler_params=pltpu.CompilerParams(
            collective_id=0, has_side_effects=True, vmem_limit_bytes=56 * 2**20
        ),
        cost_estimate=pl.CostEstimate(
            flops=2 * features * features * (4 * own + 2 * halo),
            bytes_accessed=200 * 2**20,
            transcendentals=0,
        ),
        name="weight_sums",
    )(normed_own, normed_halo, *att, *gq, *up, *ko, *kh, *vo, *vh)


def per_device(
    saved_inputs, w_query, w_key, w_value, w_out, pending, top_grads, key_blocks, counts, plan
):
    sections = lax.axis_size("section")
    section_here = lax.axis_index("section")
    part_here = lax.axis_index("mesh")
    rows_here = pending.shape[1]
    features = pending.shape[2]
    blocks_here = rows_here // BLOCK
    tick_count = plan.shape[0]
    query_weight = w_query[0]
    key_weight = w_key[0]
    value_weight = w_value[0]
    out_weight = w_out[0]
    member_ids = jnp.sum(jnp.where(jnp.arange(sections)[None, :] == section_here, plan, 0), axis=1)
    x_own = jnp.stack(
        [
            lax.dynamic_index_in_dim(saved_inputs[0], member_ids[t], 0, keepdims=False)
            for t in range(tick_count)
        ]
    )
    x_before = from_behind(x_own[:, rows_here - BLOCK :], "mesh", 1)
    x_after = from_behind(x_own[:, :BLOCK], "mesh", -1)

    positions = jnp.arange(BLOCK)
    block_ids = jnp.arange(counts.shape[0])
    global_ids = part_here * blocks_here + jnp.arange(blocks_here)
    own_count = jnp.sum(
        jnp.where(block_ids[None, :] == global_ids[:, None], counts[None, :], 0), axis=1
    )
    listed_counts = jnp.sum(
        jnp.where(block_ids[None, None, :] == key_blocks[:, :, None], counts[None, None, :], 0),
        axis=2,
    )
    near_counts = jnp.stack([listed_counts[:, 1], own_count, listed_counts[:, 0]], axis=1)
    mask = jnp.where(positions[None, None, :] < near_counts[:, :, None], 0.0, -jnp.inf)
    mask = mask.reshape(blocks_here, 3 * BLOCK).astype(jnp.float32)

    def norm(x):
        x_float = x.astype(jnp.float32)
        inv_rms = lax.rsqrt(jnp.mean(x_float * x_float, axis=-1, keepdims=True) + EPSILON)
        normed_float = x_float * inv_rms
        return inv_rms, normed_float, normed_float.astype(jnp.bfloat16)

    def project(normed, weight):
        flat = plain_dot(normed.reshape(-1, features), weight).astype(jnp.bfloat16)
        return flat.reshape(normed.shape)

    inv_rms, normed_float, normed = norm(x_own)
    queries = project(normed, query_weight)
    keys_own = project(normed, key_weight)
    values_own = project(normed, value_weight)
    normed_own_t = normed.reshape(-1, features).T
    x_halo = jnp.concatenate([x_before, x_after], axis=1)
    normed_halo = norm(x_halo)[2]
    keys_halo = project(normed_halo, key_weight)
    values_halo = project(normed_halo, value_weight)
    normed_halo_t = normed_halo.reshape(-1, features).T

    upstream = pending[0]
    outgoing = []
    stored = []
    for t in range(tick_count):
        grad_attended = right_dot(upstream, out_weight).astype(jnp.bfloat16)
        att, gq, ko, vo, kh, vh = attention(
            t, queries, keys_own, values_own, keys_halo, values_halo, grad_attended, mask
        )
        stored.append((att, gq, upstream, ko, kh, vo, vh))
        halo_term = (right_dot(kh, key_weight) + right_dot(vh, value_weight)).astype(jnp.bfloat16)
        from_after = from_behind(halo_term[:BLOCK], "mesh", -1)
        from_before = from_behind(halo_term[BLOCK:], "mesh", 1)
        grad_normed = (
            right_dot(gq, query_weight) + right_dot(ko, key_weight) + right_dot(vo, value_weight)
        )
        middle = jnp.zeros((rows_here - 2 * BLOCK, features), jnp.bfloat16)
        grad_normed = grad_normed + jnp.concatenate(
            [from_before, middle, from_after], axis=0
        ).astype(jnp.float32)
        grad_input = inv_rms[t] * (
            grad_normed
            - normed_float[t]
            * jnp.mean(grad_normed * normed_float[t], axis=-1, keepdims=True)
        )
        grad_x = (upstream.astype(jnp.float32) + grad_input).astype(jnp.bfloat16)
        outgoing.append(grad_x)
        if t + 1 < tick_count:
            passed = shifted(grad_x, "section", -1)
            upstream = jnp.where(section_here == sections - 1, top_grads[t], passed)
    layer_total = weight_sums(normed_own_t, normed_halo_t, *zip(*stored))
    return (layer_total.transpose(1, 0, 2)[None], jnp.stack(outgoing)[:, None])


def solution(mesh):
    in_specs = (
        P("section", None, "mesh", None),
        P("section", None, None),
        P("section", None, None),
        P("section", None, None),
        P("section", None, None),
        P("section", "mesh", None),
        P(None, "mesh", None),
        P("mesh", None),
        P(),
        P(),
    )
    out_specs = (P("section", "mesh", None, None), P(None, "section", "mesh", None))
    return jax.shard_map(
        per_device, mesh=mesh, in_specs=in_specs, out_specs=out_specs, check_vma=False
    )
```

```python
import functools
import math

import jax
import jax.numpy as jnp
from jax import lax
from jax.experimental import pallas as pl
from jax.experimental.pallas import tpu as pltpu
from jax.sharding import PartitionSpec as P

HEADS = 8
BLOCK = 128
OFFSETS = (1, -1)
EPSILON = 1e-06
MESH = pl.DeviceIdType.MESH


def from_behind(value, axis, steps):
    count = lax.axis_size(axis)
    pairs = [(source, (source + steps) % count) for source in range(count)]
    return lax.ppermute(value, axis, pairs)


def shifted(x, axis, by):
    size = lax.axis_size(axis)
    pairs = [(i, i + by) for i in range(size) if 0 <= i + by < size]
    return lax.ppermute(x, axis, pairs)


def right_dot(left, right):
    return lax.dot_general(
        left, right, (((1,), (1,)), ((), ())), preferred_element_type=jnp.float32
    )


def left_dot(left, right):
    return lax.dot_general(
        left, right, (((0,), (0,)), ((), ())), preferred_element_type=jnp.float32
    )


def plain_dot(left, right):
    return jnp.dot(left, right, preferred_element_type=jnp.float32)


def near_keys(own_ref, halo_ref, columns):
    return jnp.concatenate(
        [halo_ref[:BLOCK, columns], own_ref[:, columns], halo_ref[BLOCK:, columns]], axis=0
    )


def softmax(q, k, mask, scale):
    scores = right_dot(q, k) * scale + mask
    raised = jnp.exp(scores - jnp.max(scores, axis=-1, keepdims=True))
    return raised / jnp.sum(raised, axis=-1, keepdims=True)


def head_forward(scale, q_ref, ko_ref, vo_ref, kh_ref, vh_ref, mask_ref, att_ref):
    every = slice(None)
    keys = near_keys(ko_ref, kh_ref, every)
    values = near_keys(vo_ref, vh_ref, every)
    for b in range(q_ref.shape[0] // BLOCK):
        rows = slice(b * BLOCK, (b + 1) * BLOCK)
        near = slice(b * BLOCK, (b + 3) * BLOCK)
        probs = softmax(q_ref[rows], keys[near], mask_ref[b : b + 1, :], scale)
        att_ref[:, rows] = lax.dot_general(
            values[near], probs.astype(jnp.bfloat16), (((0,), (1,)), ((), ())),
            preferred_element_type=jnp.float32,
        ).astype(jnp.bfloat16)


def head_backward(
    scale, columns, q_ref, ko_ref, vo_ref, kh_ref, vh_ref, ga_ref, mask_ref,
    gq_ref, kto_ref, vto_ref, kth_ref, vth_ref, att_ref=None,
):
    size = BLOCK
    keys = near_keys(ko_ref, kh_ref, columns)
    values = near_keys(vo_ref, vh_ref, columns)
    blocks = q_ref.shape[0] // size
    key_sums = [None] * (blocks + 2)
    value_sums = [None] * (blocks + 2)
    for b in range(blocks):
        rows = slice(b * size, (b + 1) * size)
        near = slice(b * size, (b + 3) * size)
        q = q_ref[rows, columns]
        ga = ga_ref[rows, columns]
        k = keys[near]
        v = values[near]
        probs = softmax(q, k, mask_ref[b : b + 1, :], scale)
        probs_bf = probs.astype(jnp.bfloat16)
        if att_ref is not None:
            att_ref[:, rows] = lax.dot_general(
                v, probs_bf, (((0,), (1,)), ((), ())), preferred_element_type=jnp.float32
            ).astype(jnp.bfloat16)
        grad_probs = right_dot(ga, v)
        inner = jnp.sum(probs * grad_probs, axis=-1, keepdims=True)
        scores_bf = (probs * (grad_probs - inner) * scale).astype(jnp.bfloat16)
        gq_ref[rows, columns] = plain_dot(scores_bf, k).astype(jnp.bfloat16)
        key_terms = left_dot(scores_bf, q)
        value_terms = left_dot(probs_bf, ga)
        for j in range(3):
            part = slice(j * size, (j + 1) * size)
            for sums, terms in ((key_sums, key_terms), (value_sums, value_terms)):
                old = sums[b + j]
                sums[b + j] = terms[part] if old is None else old + terms[part]
    for sums, own, halo in ((key_sums, kto_ref, kth_ref), (value_sums, vto_ref, vth_ref)):
        halo[:size, columns] = sums[0].astype(jnp.bfloat16)
        halo[size:, columns] = sums[blocks + 1].astype(jnp.bfloat16)
        for b in range(blocks):
            own[b * size : (b + 1) * size, columns] = sums[b + 1].astype(jnp.bfloat16)


def turn(from_ref, to_ref):
    rows = from_ref.shape[0]
    down = lax.broadcasted_iota(jnp.int32, (rows, rows), 0)
    across = lax.broadcasted_iota(jnp.int32, (rows, rows), 1)
    identity = jnp.where(down == across, 1.0, 0.0).astype(jnp.bfloat16)
    to_ref[...] = left_dot(from_ref[...], identity).astype(jnp.bfloat16)


def forward_kernel(scale, q, ko, vo, kh, vh, mask, no, nh, att, not_, nht):
    head_forward(scale, q, ko, vo, kh, vh, mask, att)
    turn(no, not_)
    turn(nh, nht)


def both_kernel(
    scale, q, ko, vo, kh, vh, mask, no, nh, ga, att, not_, nht, gq, kto, vto, kth, vth
):
    head_backward(
        scale, slice(None), q, ko, vo, kh, vh, ga, mask, gq, kto, vto, kth, vth, att
    )
    turn(no, not_)
    turn(nh, nht)


def attention(q, ko, vo, kh, vh, mask, no, nh, ga=None):
    rows, features = q.shape
    dim = features // HEADS
    halo = kh.shape[0]
    flat = lambda n: pl.BlockSpec((n, dim), lambda h: (0, h))
    tall = lambda n: pl.BlockSpec((dim, n), lambda h: (h, 0))
    shape = lambda n: jax.ShapeDtypeStruct((n, features), jnp.bfloat16)
    tall_shape = lambda n: jax.ShapeDtypeStruct((features, n), jnp.bfloat16)
    in_specs = [flat(rows), flat(rows), flat(rows), flat(halo), flat(halo)]
    in_specs += [pl.BlockSpec(mask.shape, lambda h: (0, 0)), flat(rows), flat(halo)]
    out_specs = [tall(rows), tall(rows), tall(halo)]
    out_shape = [tall_shape(rows), tall_shape(rows), tall_shape(halo)]
    operands = [q, ko, vo, kh, vh, mask, no, nh]
    if ga is not None:
        in_specs.append(flat(rows))
        operands.append(ga)
        out_specs += [flat(rows), flat(rows), flat(rows), flat(halo), flat(halo)]
        out_shape += [shape(rows), shape(rows), shape(rows), shape(halo), shape(halo)]
    return pl.pallas_call(
        functools.partial(
            forward_kernel if ga is None else both_kernel, 1.0 / math.sqrt(dim)
        ),
        grid=(HEADS,),
        in_specs=in_specs,
        out_specs=out_specs,
        out_shape=out_shape,
        cost_estimate=pl.CostEstimate(
            flops=(4 if ga is None else 12) * rows * 3 * BLOCK * features,
            bytes_accessed=24 * rows * features,
            transcendentals=rows * 3 * BLOCK * HEADS,
        ),
        name="attention_forward" if ga is None else "attention_both_ways",
    )(*operands)


def bit_orders(bits):
    swapped = [1, 0] + list(range(2, bits))
    late = list(range(2, bits)) + [0, 1]
    return (list(range(bits)), swapped, late)


QUARTERS = 4
PORTIONS = ((3, 0, 0), (3, 1, 1), (3, 2, 2), (3, 3, 2)) + tuple(
    (projection, quarter, quarter % 2) for projection in range(3) for quarter in range(QUARTERS)
)
EARLY = 4


def last_kernel(
    count, n0, nh0, n1, nh1, att0, att1, gq0, ko0, vo0, kh0, vh0, up0, up1,
    q1, key1, value1, key_halo1, value_halo1, mask, x1, wq, wk, wv, wo,
    out_ref, grad_x_ref,
    nlhs, alhs, keep, send, recv, ga1, gq1, ko1, vo1, kh1, vh1, term, term_in,
    send_sem, recv_sem, term_send, term_recv,
):
    me = lax.axis_index("mesh")
    bits = count.bit_length() - 1
    orders = bit_orders(bits)
    features = n0.shape[0]
    rows_here = x1.shape[0]
    chunk = features // count
    width = features // QUARTERS
    scale = 1.0 / math.sqrt(features // HEADS)
    after = lax.rem(me + 1, count)
    before = lax.rem(me + count - 1, count)

    def bit_of(b):
        return lax.rem(me // (1 << b), 2)

    def partner(b):
        return me + (1 - 2 * bit_of(b)) * (1 << b)

    barrier = pltpu.get_barrier_semaphore()
    for other in [before, after] + [partner(b) for b in range(bits)]:
        pl.semaphore_signal(barrier, inc=1, device_id={"mesh": other}, device_id_type=MESH)

    def chunk_rows(order, place):
        index = 0
        for k, b in enumerate(order):
            here = bit_of(b)
            flip = (place >> (bits - 1 - k)) & 1
            index = index + (1 - here if flip else here) * (1 << b)
        return pl.ds(pl.multiple_of(index * chunk, chunk), chunk)

    def arrange(to_ref, slot, order, parts):
        for place in range(count):
            rows = chunk_rows(order, place)
            first = 0
            for part in parts:
                last = first + part.shape[1]
                to_ref[slot, place * chunk : (place + 1) * chunk, first:last] = part[rows, :]
                first = last

    rights = ((gq0, gq1), (ko0, ko1, kh0, kh1), (vo0, vo1, vh0, vh1), (up0, up1))

    def columns_of(portion):
        return slice(portion[1] * width, (portion[1] + 1) * width)

    def product(portion, rows):
        projection, _, order = portion
        right = jnp.concatenate([r[:, columns_of(portion)] for r in rights[projection]], axis=0)
        left = alhs if projection == 3 else nlhs
        return plain_dot(left[order, rows, : right.shape[0]], right)

    starts = []
    first = 0
    for k in range(bits):
        starts.append(first)
        first += features >> (k + 1)

    def copy_of(p, k):
        rows = pl.ds(starts[k], features >> (k + 1))
        return pltpu.make_async_remote_copy(
            src_ref=send.at[p, rows],
            dst_ref=recv.at[p, rows],
            send_sem=send_sem.at[p, k],
            recv_sem=recv_sem.at[p, k],
            device_id={"mesh": partner(orders[PORTIONS[p][2]][k])},
            device_id_type=MESH,
        )

    def term_copy(side):
        return pltpu.make_async_remote_copy(
            src_ref=term.at[pl.ds(side * BLOCK, BLOCK)],
            dst_ref=term_in.at[pl.ds((1 - side) * BLOCK, BLOCK)],
            send_sem=term_send.at[side],
            recv_sem=term_recv.at[1 - side],
            device_id={"mesh": after if side else before},
            device_id_type=MESH,
        )

    def arrived(side):
        return term_copy(1 - side)

    middle = features // 2

    def begin(p):
        send[p, :middle] = product(PORTIONS[p], slice(middle, features)).astype(jnp.bfloat16)
        copy_of(p, 0).start()

    for slot, order in enumerate(orders):
        arrange(alhs, slot, order, (att0, att1))
    pl.semaphore_wait(barrier, bits + 2)
    for p in range(EARLY):
        begin(p)

    ga1[...] = right_dot(up1[...], wo[...]).astype(jnp.bfloat16)
    dim = features // HEADS

    @pl.loop(0, HEADS)
    def _(h):
        columns = pl.ds(pl.multiple_of(h * dim, dim), dim)
        head_backward(
            scale, columns, q1, key1, value1, key_halo1, value_halo1, ga1, mask,
            gq1, ko1, vo1, kh1, vh1,
        )

    term[...] = (right_dot(kh1[...], wk[...]) + right_dot(vh1[...], wv[...])).astype(jnp.bfloat16)
    for side in (0, 1):
        term_copy(side).start()
    for slot in (0, 1):
        arrange(nlhs, slot, orders[slot], (n0, n1, nh0, nh1))
    for p in range(EARLY, len(PORTIONS)):
        begin(p)
    for p, portion in enumerate(PORTIONS):
        keep[p] = product(portion, slice(0, middle))

    def finish_input():
        x_float = x1[...].astype(jnp.float32)
        inv_rms = lax.rsqrt(jnp.mean(x_float * x_float, axis=-1, keepdims=True) + EPSILON)
        normed = x_float * inv_rms
        grad = right_dot(gq1[...], wq[...])
        grad = grad + right_dot(ko1[...], wk[...]) + right_dot(vo1[...], wv[...])
        for side in (0, 1):
            arrived(side).wait_recv()
        pieces = [term_in[:BLOCK].astype(jnp.float32)]
        if rows_here > 2 * BLOCK:
            pieces.append(jnp.zeros((rows_here - 2 * BLOCK, features), jnp.float32))
        pieces.append(term_in[BLOCK:].astype(jnp.float32))
        grad = grad + jnp.concatenate(pieces, axis=0)
        grad = inv_rms * (grad - normed * jnp.mean(grad * normed, axis=-1, keepdims=True))
        grad_x_ref[...] = (up1[...].astype(jnp.float32) + grad).astype(jnp.bfloat16)

    for k in range(bits):
        size = features >> (k + 1)
        for p, portion in enumerate(PORTIONS):
            copy_of(p, k).wait_recv()
            if k + 1 < bits:
                left = size // 2
                send[p, starts[k + 1] : starts[k + 1] + left] = (
                    keep[p, left:size]
                    + recv[p, starts[k] + left : starts[k] + size].astype(jnp.float32)
                ).astype(jnp.bfloat16)
                copy_of(p, k + 1).start()
                keep[p, :left] += recv[p, starts[k] : starts[k] + left].astype(jnp.float32)
            else:
                out_ref[:, portion[0], columns_of(portion)] = keep[p, :size] + recv[
                    p, starts[k] : starts[k] + size
                ].astype(jnp.float32)
        if k == 0:
            finish_input()
    for k in range(bits):
        for p in range(len(PORTIONS)):
            copy_of(p, k).wait_send()
    for side in (0, 1):
        term_copy(side).wait_send()


def last_tick(*operands):
    count = lax.axis_size("mesh")
    bits = count.bit_length() - 1
    features, rows = operands[0].shape
    halo = operands[1].shape[1]
    chunk = features // count
    portions = len(PORTIONS)
    moved = features - chunk
    width = features // QUARTERS
    half = lambda *shape: pltpu.VMEM(shape, jnp.bfloat16)
    return pl.pallas_call(
        functools.partial(last_kernel, count),
        out_shape=[
            jax.ShapeDtypeStruct((chunk, 4, features), jnp.float32),
            jax.ShapeDtypeStruct((rows, features), jnp.bfloat16),
        ],
        in_specs=[pl.BlockSpec(memory_space=pltpu.VMEM)] * len(operands),
        out_specs=[pl.BlockSpec(memory_space=pltpu.VMEM)] * 2,
        scratch_shapes=[
            half(2, features, 2 * (rows + halo)),
            half(3, features, 2 * rows),
            pltpu.VMEM((portions, features // 2, width), jnp.float32),
            half(portions, moved, width),
            half(portions, moved, width),
            half(rows, features),
            half(rows, features),
            half(rows, features),
            half(rows, features),
            half(halo, features),
            half(halo, features),
            half(halo, features),
            half(halo, features),
            pltpu.SemaphoreType.DMA((portions, bits)),
            pltpu.SemaphoreType.DMA((portions, bits)),
            pltpu.SemaphoreType.DMA((2,)),
            pltpu.SemaphoreType.DMA((2,)),
        ],
        compiler_params=pltpu.CompilerParams(
            collective_id=0, has_side_effects=True, vmem_limit_bytes=60 * 2**20
        ),
        cost_estimate=pl.CostEstimate(
            flops=4 * features * features * (4 * rows + 2 * halo),
            bytes_accessed=200 * 2**20,
            transcendentals=0,
        ),
        name="last_tick",
    )(*operands)


def per_device(
    saved_inputs, w_query, w_key, w_value, w_out, pending, top_grads, key_blocks, counts, plan
):
    sections = lax.axis_size("section")
    section_here = lax.axis_index("section")
    part_here = lax.axis_index("mesh")
    rows_here = pending.shape[1]
    features = pending.shape[2]
    blocks_here = rows_here // BLOCK
    query_weight = w_query[0]
    key_weight = w_key[0]
    value_weight = w_value[0]
    out_weight = w_out[0]

    def norm(x):
        x_float = x.astype(jnp.float32)
        inv_rms = lax.rsqrt(jnp.mean(x_float * x_float, axis=-1, keepdims=True) + EPSILON)
        normed_float = x_float * inv_rms
        return inv_rms, normed_float, normed_float.astype(jnp.bfloat16)

    def project(normed, weight):
        return plain_dot(normed, weight).astype(jnp.bfloat16)

    members = lax.dynamic_index_in_dim(plan, section_here, 1, keepdims=False)
    inputs = [
        lax.dynamic_index_in_dim(saved_inputs[0], members[t], 0, keepdims=False) for t in (0, 1)
    ]
    halos = [
        jnp.concatenate(
            [
                from_behind(x[rows_here - BLOCK :], "mesh", 1),
                from_behind(x[:BLOCK], "mesh", -1),
            ],
            axis=0,
        )
        for x in inputs
    ]

    positions = jnp.arange(BLOCK)
    block_ids = jnp.arange(counts.shape[0])
    global_ids = part_here * blocks_here + jnp.arange(blocks_here)
    near_ids = jnp.stack([key_blocks[:, 1], global_ids, key_blocks[:, 0]], axis=1)
    near_counts = jnp.sum(
        jnp.where(block_ids[None, None, :] == near_ids[:, :, None], counts[None, None, :], 0),
        axis=2,
    )
    mask = jnp.where(positions[None, None, :] < near_counts[:, :, None], 0.0, -jnp.inf)
    mask = mask.reshape(blocks_here, 3 * BLOCK).astype(jnp.float32)

    def ready(t):
        normed = norm(inputs[t])[2]
        own = [project(normed, w) for w in (query_weight, key_weight, value_weight)]
        normed_halo = norm(halos[t])[2]
        near = [project(normed_halo, w) for w in (key_weight, value_weight)]
        return own + near + [mask, normed, normed_halo]

    upstream = pending[0]
    first = ready(0)
    second = ready(1)
    grad_attended = right_dot(upstream, out_weight).astype(jnp.bfloat16)
    att0, n0, nh0, gq, ko, vo, kh, vh = attention(*first, grad_attended)
    halo_term = (right_dot(kh, key_weight) + right_dot(vh, value_weight)).astype(jnp.bfloat16)
    from_after = from_behind(halo_term[:BLOCK], "mesh", -1)
    from_before = from_behind(halo_term[BLOCK:], "mesh", 1)
    att1, n1, nh1 = attention(*second)
    grad_normed = (
        right_dot(gq, query_weight) + right_dot(ko, key_weight) + right_dot(vo, value_weight)
    )
    middle = jnp.zeros((rows_here - 2 * BLOCK, features), jnp.bfloat16)
    grad_normed = grad_normed + jnp.concatenate([from_before, middle, from_after], axis=0).astype(
        jnp.float32
    )
    inv_rms, normed_float, _ = norm(inputs[0])
    grad_input = inv_rms * (
        grad_normed - normed_float * jnp.mean(grad_normed * normed_float, axis=-1, keepdims=True)
    )
    grad_x = (upstream.astype(jnp.float32) + grad_input).astype(jnp.bfloat16)
    passed = shifted(grad_x, "section", -1)
    later = jnp.where(section_here == sections - 1, top_grads[0], passed)
    layer_total, grad_x_last = last_tick(
        n0, nh0, n1, nh1, att0, att1, gq, ko, vo, kh, vh, upstream, later,
        *second[:6], inputs[1], query_weight, key_weight, value_weight, out_weight,
    )
    return (layer_total[None], jnp.stack([grad_x, grad_x_last])[:, None])


def solution(mesh):
    in_specs = (
        P("section", None, "mesh", None),
        P("section", None, None),
        P("section", None, None),
        P("section", None, None),
        P("section", None, None),
        P("section", "mesh", None),
        P(None, "mesh", None),
        P("mesh", None),
        P(),
        P(),
    )
    out_specs = (P("section", "mesh", None, None), P(None, "section", "mesh", None))
    return jax.shard_map(
        per_device, mesh=mesh, in_specs=in_specs, out_specs=out_specs, check_vma=False
    )
```

```python
import functools
import math

import jax
import jax.numpy as jnp
from jax import lax
from jax.experimental import pallas as pl
from jax.experimental.pallas import tpu as pltpu
from jax.sharding import PartitionSpec as P

HEADS = 8
BLOCK = 128
GROUP = 2
OFFSETS = (1, -1)
EPSILON = 1e-06
MESH = pl.DeviceIdType.MESH


def from_behind(value, axis, steps):
    count = lax.axis_size(axis)
    pairs = [(source, (source + steps) % count) for source in range(count)]
    return lax.ppermute(value, axis, pairs)


def shifted(x, axis, by):
    size = lax.axis_size(axis)
    pairs = [(i, i + by) for i in range(size) if 0 <= i + by < size]
    return lax.ppermute(x, axis, pairs)


def right_dot(left, right):
    return lax.dot_general(
        left, right, (((1,), (1,)), ((), ())), preferred_element_type=jnp.float32
    )


def left_dot(left, right):
    return lax.dot_general(
        left, right, (((0,), (0,)), ((), ())), preferred_element_type=jnp.float32
    )


def plain_dot(left, right):
    return jnp.dot(left, right, preferred_element_type=jnp.float32)


def near_keys(own_ref, halo_ref, columns):
    return jnp.concatenate(
        [halo_ref[:BLOCK, columns], own_ref[:, columns], halo_ref[BLOCK:, columns]], axis=0
    )


def softmax(q, k, mask, scale):
    scores = right_dot(q, k) * scale + mask
    raised = jnp.exp(scores - jnp.max(scores, axis=-1, keepdims=True))
    return raised * (1.0 / jnp.sum(raised, axis=-1, keepdims=True))


def head_forward(scale, columns, q_ref, ko_ref, vo_ref, kh_ref, vh_ref, mask_ref, att_ref):
    keys = near_keys(ko_ref, kh_ref, columns)
    values = near_keys(vo_ref, vh_ref, columns)
    for b in range(q_ref.shape[0] // BLOCK):
        rows = slice(b * BLOCK, (b + 1) * BLOCK)
        near = slice(b * BLOCK, (b + 3) * BLOCK)
        probs = softmax(q_ref[rows, columns], keys[near], mask_ref[b : b + 1, :], scale)
        att_ref[columns, rows] = lax.dot_general(
            values[near], probs.astype(jnp.bfloat16), (((0,), (1,)), ((), ())),
            preferred_element_type=jnp.float32,
        ).astype(jnp.bfloat16)


def head_backward(
    scale, columns, q_ref, ko_ref, vo_ref, kh_ref, vh_ref, ga_ref, mask_ref,
    gq_ref, kto_ref, vto_ref, kth_ref, vth_ref, att_ref=None,
):
    size = BLOCK
    keys = near_keys(ko_ref, kh_ref, columns)
    values = near_keys(vo_ref, vh_ref, columns)
    blocks = q_ref.shape[0] // size
    key_sums = [None] * (blocks + 2)
    value_sums = [None] * (blocks + 2)
    for b in range(blocks):
        rows = slice(b * size, (b + 1) * size)
        near = slice(b * size, (b + 3) * size)
        q = q_ref[rows, columns]
        ga = ga_ref[rows, columns]
        k = keys[near]
        v = values[near]
        probs = softmax(q, k, mask_ref[b : b + 1, :], scale)
        probs_bf = probs.astype(jnp.bfloat16)
        if att_ref is not None:
            att_ref[columns, rows] = lax.dot_general(
                v, probs_bf, (((0,), (1,)), ((), ())), preferred_element_type=jnp.float32
            ).astype(jnp.bfloat16)
        grad_probs = right_dot(ga, v)
        inner = jnp.sum(probs * grad_probs, axis=-1, keepdims=True)
        scores_bf = (probs * (grad_probs - inner) * scale).astype(jnp.bfloat16)
        gq_ref[rows, columns] = plain_dot(scores_bf, k).astype(jnp.bfloat16)
        key_terms = left_dot(scores_bf, q)
        value_terms = left_dot(probs_bf, ga)
        for j in range(3):
            part = slice(j * size, (j + 1) * size)
            for sums, terms in ((key_sums, key_terms), (value_sums, value_terms)):
                old = sums[b + j]
                sums[b + j] = terms[part] if old is None else old + terms[part]
    for sums, own, halo in ((key_sums, kto_ref, kth_ref), (value_sums, vto_ref, vth_ref)):
        halo[:size, columns] = sums[0].astype(jnp.bfloat16)
        halo[size:, columns] = sums[blocks + 1].astype(jnp.bfloat16)
        for b in range(blocks):
            own[b * size : (b + 1) * size, columns] = sums[b + 1].astype(jnp.bfloat16)


def turn(from_ref, to_ref):
    rows = from_ref.shape[0]
    down = lax.broadcasted_iota(jnp.int32, (rows, rows), 0)
    across = lax.broadcasted_iota(jnp.int32, (rows, rows), 1)
    identity = jnp.where(down == across, 1.0, 0.0).astype(jnp.bfloat16)
    to_ref[...] = left_dot(from_ref[...], identity).astype(jnp.bfloat16)


def heads_of(q, scale):
    dim = round(1.0 / scale**2)
    return [slice(first, first + dim) for first in range(0, q.shape[1], dim)]


def forward_kernel(scale, q, ko, vo, kh, vh, mask, no, nh, att, not_, nht):
    for columns in heads_of(q, scale):
        head_forward(scale, columns, q, ko, vo, kh, vh, mask, att)
    turn(no, not_)
    turn(nh, nht)


def both_kernel(
    scale, q, ko, vo, kh, vh, mask, no, nh, ga, att, not_, nht, gq, kto, vto, kth, vth
):
    for columns in heads_of(q, scale):
        head_backward(scale, columns, q, ko, vo, kh, vh, ga, mask, gq, kto, vto, kth, vth, att)
    turn(no, not_)
    turn(nh, nht)


def attention(q, ko, vo, kh, vh, mask, no, nh, ga=None):
    rows, features = q.shape
    dim = features // HEADS
    halo = kh.shape[0]
    flat = lambda n: pl.BlockSpec((n, GROUP * dim), lambda h: (0, h))
    tall = lambda n: pl.BlockSpec((GROUP * dim, n), lambda h: (h, 0))
    shape = lambda n: jax.ShapeDtypeStruct((n, features), jnp.bfloat16)
    tall_shape = lambda n: jax.ShapeDtypeStruct((features, n), jnp.bfloat16)
    in_specs = [flat(rows), flat(rows), flat(rows), flat(halo), flat(halo)]
    in_specs += [pl.BlockSpec(mask.shape, lambda h: (0, 0)), flat(rows), flat(halo)]
    out_specs = [tall(rows), tall(rows), tall(halo)]
    out_shape = [tall_shape(rows), tall_shape(rows), tall_shape(halo)]
    operands = [q, ko, vo, kh, vh, mask, no, nh]
    if ga is not None:
        in_specs.append(flat(rows))
        operands.append(ga)
        out_specs += [flat(rows), flat(rows), flat(rows), flat(halo), flat(halo)]
        out_shape += [shape(rows), shape(rows), shape(rows), shape(halo), shape(halo)]
    return pl.pallas_call(
        functools.partial(
            forward_kernel if ga is None else both_kernel, 1.0 / math.sqrt(dim)
        ),
        grid=(HEADS // GROUP,),
        in_specs=in_specs,
        out_specs=out_specs,
        out_shape=out_shape,
        cost_estimate=pl.CostEstimate(
            flops=(4 if ga is None else 12) * rows * 3 * BLOCK * features,
            bytes_accessed=24 * rows * features,
            transcendentals=rows * 3 * BLOCK * HEADS,
        ),
        name="attention_forward" if ga is None else "attention_both_ways",
    )(*operands)


def bit_orders(bits):
    swapped = [1, 0] + list(range(2, bits))
    late = list(range(2, bits)) + [0, 1]
    return (list(range(bits)), swapped, late)


QUARTERS = 4
PORTIONS = ((3, 0, 0), (3, 1, 1), (3, 2, 2), (3, 3, 2)) + tuple(
    (projection, quarter, quarter % 2) for projection in range(3) for quarter in range(QUARTERS)
)
EARLY = 4
LAG = 2


def last_kernel(
    count, n0, nh0, n1, nh1, att0, att1, gq0, ko0, vo0, kh0, vh0, up0, up1,
    q1, key1, value1, key_halo1, value_halo1, mask, x1, wq, wk, wv, wo, grad_x0,
    out_ref, grad_x_ref,
    nlhs, alhs, keep, send, recv, ga1, gq1, ko1, vo1, kh1, vh1, term, term_in,
    send_sem, recv_sem, term_send, term_recv,
):
    me = lax.axis_index("mesh")
    bits = count.bit_length() - 1
    orders = bit_orders(bits)
    features = n0.shape[0]
    rows_here = x1.shape[0]
    chunk = features // count
    width = features // QUARTERS
    scale = 1.0 / math.sqrt(features // HEADS)
    after = lax.rem(me + 1, count)
    before = lax.rem(me + count - 1, count)

    def bit_of(b):
        return lax.rem(me // (1 << b), 2)

    def partner(b):
        return me + (1 - 2 * bit_of(b)) * (1 << b)

    barrier = pltpu.get_barrier_semaphore()
    for other in [before, after] + [partner(b) for b in range(bits)]:
        pl.semaphore_signal(barrier, inc=1, device_id={"mesh": other}, device_id_type=MESH)

    def chunk_rows(order, place):
        index = 0
        for k, b in enumerate(order):
            here = bit_of(b)
            flip = (place >> (bits - 1 - k)) & 1
            index = index + (1 - here if flip else here) * (1 << b)
        return pl.ds(pl.multiple_of(index * chunk, chunk), chunk)

    def arrange(to_ref, slot, order, parts):
        for place in range(count):
            rows = chunk_rows(order, place)
            first = 0
            for part in parts:
                last = first + part.shape[1]
                to_ref[slot, place * chunk : (place + 1) * chunk, first:last] = part[rows, :]
                first = last

    rights = ((gq0, gq1), (ko0, ko1, kh0, kh1), (vo0, vo1, vh0, vh1), (up0, up1))

    def columns_of(portion):
        return slice(portion[1] * width, (portion[1] + 1) * width)

    def product(portion, rows):
        projection, _, order = portion
        right = jnp.concatenate([r[:, columns_of(portion)] for r in rights[projection]], axis=0)
        left = alhs if projection == 3 else nlhs
        return plain_dot(left[order, rows, : right.shape[0]], right)

    starts = []
    first = 0
    for k in range(bits):
        starts.append(first)
        first += features >> (k + 1)

    def copy_of(p, k):
        rows = pl.ds(starts[k], features >> (k + 1))
        return pltpu.make_async_remote_copy(
            src_ref=send.at[p, rows],
            dst_ref=recv.at[p, rows],
            send_sem=send_sem.at[p, k],
            recv_sem=recv_sem.at[p, k],
            device_id={"mesh": partner(orders[PORTIONS[p][2]][k])},
            device_id_type=MESH,
        )

    def term_copy(side):
        return pltpu.make_async_remote_copy(
            src_ref=term.at[pl.ds(side * BLOCK, BLOCK)],
            dst_ref=term_in.at[pl.ds((1 - side) * BLOCK, BLOCK)],
            send_sem=term_send.at[side],
            recv_sem=term_recv.at[1 - side],
            device_id={"mesh": after if side else before},
            device_id_type=MESH,
        )

    def arrived(side):
        return term_copy(1 - side)

    middle = features // 2

    def begin(p):
        send[p, :middle] = product(PORTIONS[p], slice(middle, features)).astype(jnp.bfloat16)
        copy_of(p, 0).start()

    for slot, order in enumerate(orders):
        arrange(alhs, slot, order, (att0, att1))
    pl.semaphore_wait(barrier, bits + 2)
    for p in range(EARLY):
        begin(p)

    ga1[...] = right_dot(up1[...], wo[...]).astype(jnp.bfloat16)
    dim = features // HEADS

    def heads(first, last):
        @pl.loop(first, last)
        def _(pair):
            for h in range(GROUP):
                columns = pl.ds(pl.multiple_of((pair * GROUP + h) * dim, dim), dim)
                head_backward(
                    scale, columns, q1, key1, value1, key_halo1, value_halo1, ga1, mask,
                    gq1, ko1, vo1, kh1, vh1,
                )

    def advance(p, k):
        portion = PORTIONS[p]
        size = features >> (k + 1)
        if k == 0:
            keep[p] = product(portion, slice(0, middle))
        copy_of(p, k).wait_recv()
        if k + 1 < bits:
            left = size // 2
            send[p, starts[k + 1] : starts[k + 1] + left] = (
                keep[p, left:size]
                + recv[p, starts[k] + left : starts[k] + size].astype(jnp.float32)
            ).astype(jnp.bfloat16)
            copy_of(p, k + 1).start()
            keep[p, :left] += recv[p, starts[k] : starts[k] + left].astype(jnp.float32)
        else:
            out_ref[:, portion[0], columns_of(portion)] = keep[p, :size] + recv[
                p, starts[k] : starts[k] + size
            ].astype(jnp.float32)

    groups = HEADS // GROUP
    done = 0
    for k, last in enumerate((groups // 2, 3 * groups // 4, groups)):
        heads(done, last)
        done = last
        for p in range(EARLY):
            advance(p, k)

    term[...] = (right_dot(kh1[...], wk[...]) + right_dot(vh1[...], wv[...])).astype(jnp.bfloat16)
    for side in (0, 1):
        term_copy(side).start()
    for slot in (0, 1):
        arrange(nlhs, slot, orders[slot], (n0, n1, nh0, nh1))
    for p in range(EARLY, len(PORTIONS)):
        begin(p)
    def finish_input():
        x_float = x1[...].astype(jnp.float32)
        inv_rms = lax.rsqrt(jnp.mean(x_float * x_float, axis=-1, keepdims=True) + EPSILON)
        normed = x_float * inv_rms
        grad = right_dot(gq1[...], wq[...])
        grad = grad + right_dot(ko1[...], wk[...]) + right_dot(vo1[...], wv[...])
        for side in (0, 1):
            arrived(side).wait_recv()
        pieces = [term_in[:BLOCK].astype(jnp.float32)]
        if rows_here > 2 * BLOCK:
            pieces.append(jnp.zeros((rows_here - 2 * BLOCK, features), jnp.float32))
        pieces.append(term_in[BLOCK:].astype(jnp.float32))
        grad = grad + jnp.concatenate(pieces, axis=0)
        grad = inv_rms * (grad - normed * jnp.mean(grad * normed, axis=-1, keepdims=True))
        grad_x_ref[0] = grad_x0[...]
        grad_x_ref[1] = (up1[...].astype(jnp.float32) + grad).astype(jnp.bfloat16)

    for p in range(EARLY):
        for k in range(3, bits):
            advance(p, k)
    rest = range(EARLY, len(PORTIONS))
    for stage in range(len(rest) + LAG * (bits - 1)):
        for k in reversed(range(bits)):
            place = stage - LAG * k
            if 0 <= place < len(rest):
                advance(rest[place], k)
        if stage == LAG:
            finish_input()
    for k in range(bits):
        for p in range(len(PORTIONS)):
            copy_of(p, k).wait_send()
    for side in (0, 1):
        term_copy(side).wait_send()


def last_tick(*operands):
    count = lax.axis_size("mesh")
    bits = count.bit_length() - 1
    features, rows = operands[0].shape
    halo = operands[1].shape[1]
    chunk = features // count
    portions = len(PORTIONS)
    moved = features - chunk
    width = features // QUARTERS
    half = lambda *shape: pltpu.VMEM(shape, jnp.bfloat16)
    return pl.pallas_call(
        functools.partial(last_kernel, count),
        out_shape=[
            jax.ShapeDtypeStruct((chunk, 4, features), jnp.float32),
            jax.ShapeDtypeStruct((2, rows, features), jnp.bfloat16),
        ],
        in_specs=[pl.BlockSpec(memory_space=pltpu.VMEM)] * len(operands),
        out_specs=[pl.BlockSpec(memory_space=pltpu.VMEM)] * 2,
        scratch_shapes=[
            half(2, features, 2 * (rows + halo)),
            half(3, features, 2 * rows),
            pltpu.VMEM((portions, features // 2, width), jnp.float32),
            half(portions, moved, width),
            half(portions, moved, width),
            half(rows, features),
            half(rows, features),
            half(rows, features),
            half(rows, features),
            half(halo, features),
            half(halo, features),
            half(halo, features),
            half(halo, features),
            pltpu.SemaphoreType.DMA((portions, bits)),
            pltpu.SemaphoreType.DMA((portions, bits)),
            pltpu.SemaphoreType.DMA((2,)),
            pltpu.SemaphoreType.DMA((2,)),
        ],
        compiler_params=pltpu.CompilerParams(
            collective_id=0, has_side_effects=True, vmem_limit_bytes=60 * 2**20
        ),
        cost_estimate=pl.CostEstimate(
            flops=4 * features * features * (4 * rows + 2 * halo),
            bytes_accessed=200 * 2**20,
            transcendentals=0,
        ),
        name="last_tick",
    )(*operands)


def per_device(
    saved_inputs, w_query, w_key, w_value, w_out, pending, top_grads, key_blocks, counts, plan
):
    sections = lax.axis_size("section")
    section_here = lax.axis_index("section")
    part_here = lax.axis_index("mesh")
    rows_here = pending.shape[1]
    features = pending.shape[2]
    blocks_here = rows_here // BLOCK
    query_weight = w_query[0]
    key_weight = w_key[0]
    value_weight = w_value[0]
    out_weight = w_out[0]

    def norm(x):
        x_float = x.astype(jnp.float32)
        inv_rms = lax.rsqrt(jnp.mean(x_float * x_float, axis=-1, keepdims=True) + EPSILON)
        normed_float = x_float * inv_rms
        return inv_rms, normed_float, normed_float.astype(jnp.bfloat16)

    def project(normed, weight):
        return plain_dot(normed, weight).astype(jnp.bfloat16)

    members = lax.dynamic_index_in_dim(plan, section_here, 1, keepdims=False)
    inputs = [
        lax.dynamic_index_in_dim(saved_inputs[0], members[t], 0, keepdims=False) for t in (0, 1)
    ]
    halos = [
        jnp.concatenate(
            [
                from_behind(x[rows_here - BLOCK :], "mesh", 1),
                from_behind(x[:BLOCK], "mesh", -1),
            ],
            axis=0,
        )
        for x in inputs
    ]

    positions = jnp.arange(BLOCK)
    block_ids = jnp.arange(counts.shape[0])
    global_ids = part_here * blocks_here + jnp.arange(blocks_here)
    near_ids = jnp.stack([key_blocks[:, 1], global_ids, key_blocks[:, 0]], axis=1)
    near_counts = jnp.sum(
        jnp.where(block_ids[None, None, :] == near_ids[:, :, None], counts[None, None, :], 0),
        axis=2,
    )
    mask = jnp.where(positions[None, None, :] < near_counts[:, :, None], 0.0, -jnp.inf)
    mask = mask.reshape(blocks_here, 3 * BLOCK).astype(jnp.float32)

    def ready(t):
        normed = norm(inputs[t])[2]
        own = [project(normed, w) for w in (query_weight, key_weight, value_weight)]
        normed_halo = norm(halos[t])[2]
        near = [project(normed_halo, w) for w in (key_weight, value_weight)]
        return own + near + [mask, normed, normed_halo]

    upstream = pending[0]
    first = ready(0)
    grad_attended = right_dot(upstream, out_weight).astype(jnp.bfloat16)
    att0, n0, nh0, gq, ko, vo, kh, vh = attention(*first, grad_attended)
    halo_term = (right_dot(kh, key_weight) + right_dot(vh, value_weight)).astype(jnp.bfloat16)
    halo_term, halos[1] = lax.optimization_barrier((halo_term, halos[1]))
    from_after = from_behind(halo_term[:BLOCK], "mesh", -1)
    from_before = from_behind(halo_term[BLOCK:], "mesh", 1)
    second = ready(1)
    att1, n1, nh1 = attention(*second)
    from_after, from_before, att1 = lax.optimization_barrier((from_after, from_before, att1))
    grad_normed = (
        right_dot(gq, query_weight) + right_dot(ko, key_weight) + right_dot(vo, value_weight)
    )
    middle = jnp.zeros((rows_here - 2 * BLOCK, features), jnp.bfloat16)
    grad_normed = grad_normed + jnp.concatenate([from_before, middle, from_after], axis=0).astype(
        jnp.float32
    )
    inv_rms, normed_float, _ = norm(inputs[0])
    grad_input = inv_rms * (
        grad_normed - normed_float * jnp.mean(grad_normed * normed_float, axis=-1, keepdims=True)
    )
    grad_x = (upstream.astype(jnp.float32) + grad_input).astype(jnp.bfloat16)
    passed = shifted(grad_x, "section", -1)
    later = jnp.where(section_here == sections - 1, top_grads[0], passed)
    layer_total, input_grads = last_tick(
        n0, nh0, n1, nh1, att0, att1, gq, ko, vo, kh, vh, upstream, later,
        *second[:6], inputs[1], query_weight, key_weight, value_weight, out_weight, grad_x,
    )
    return (layer_total[None], input_grads[:, None])


def solution(mesh):
    in_specs = (
        P("section", None, "mesh", None),
        P("section", None, None),
        P("section", None, None),
        P("section", None, None),
        P("section", None, None),
        P("section", "mesh", None),
        P(None, "mesh", None),
        P("mesh", None),
        P(),
        P(),
    )
    out_specs = (P("section", "mesh", None, None), P(None, "section", "mesh", None))
    return jax.shard_map(
        per_device, mesh=mesh, in_specs=in_specs, out_specs=out_specs, check_vma=False
    )
```

```python
import functools
import math

import jax
import jax.numpy as jnp
from jax import lax
from jax.experimental import pallas as pl
from jax.experimental.pallas import tpu as pltpu
from jax.sharding import PartitionSpec as P

HEADS = 8
BLOCK = 128
GROUP = 2
OFFSETS = (1, -1)
EPSILON = 1e-06
MESH = pl.DeviceIdType.MESH


def from_behind(value, axis, steps):
    count = lax.axis_size(axis)
    pairs = [(source, (source + steps) % count) for source in range(count)]
    return lax.ppermute(value, axis, pairs)


def shifted(x, axis, by):
    size = lax.axis_size(axis)
    pairs = [(i, i + by) for i in range(size) if 0 <= i + by < size]
    return lax.ppermute(x, axis, pairs)


def right_dot(left, right):
    return lax.dot_general(
        left, right, (((1,), (1,)), ((), ())), preferred_element_type=jnp.float32
    )


def left_dot(left, right):
    return lax.dot_general(
        left, right, (((0,), (0,)), ((), ())), preferred_element_type=jnp.float32
    )


def plain_dot(left, right):
    return jnp.dot(left, right, preferred_element_type=jnp.float32)


def near_keys(own_ref, halo_ref, columns):
    return jnp.concatenate(
        [halo_ref[:BLOCK, columns], own_ref[:, columns], halo_ref[BLOCK:, columns]], axis=0
    )


def softmax(q, k, mask, scale):
    scores = right_dot(k, q) * scale + mask
    raised = jnp.exp(scores - jnp.max(scores, axis=0, keepdims=True))
    return raised * (1.0 / jnp.sum(raised, axis=0, keepdims=True))


def head_forward(scale, columns, q_ref, ko_ref, vo_ref, kh_ref, vh_ref, mask_ref, att_ref):
    keys = near_keys(ko_ref, kh_ref, columns)
    values = near_keys(vo_ref, vh_ref, columns)
    for b in range(q_ref.shape[0] // BLOCK):
        rows = slice(b * BLOCK, (b + 1) * BLOCK)
        near = slice(b * BLOCK, (b + 3) * BLOCK)
        probs = softmax(q_ref[rows, columns], keys[near], mask_ref[3 * b * BLOCK : 3 * (b + 1) * BLOCK, :], scale)
        att_ref[columns, rows] = left_dot(values[near], probs.astype(jnp.bfloat16)).astype(
            jnp.bfloat16
        )


def head_backward(
    scale, columns, q_ref, ko_ref, vo_ref, kh_ref, vh_ref, ga_ref, mask_ref,
    gq_ref, kto_ref, vto_ref, kth_ref, vth_ref, att_ref=None,
):
    size = BLOCK
    keys = near_keys(ko_ref, kh_ref, columns)
    values = near_keys(vo_ref, vh_ref, columns)
    blocks = q_ref.shape[0] // size
    key_sums = [None] * (blocks + 2)
    value_sums = [None] * (blocks + 2)
    for b in range(blocks):
        rows = slice(b * size, (b + 1) * size)
        near = slice(b * size, (b + 3) * size)
        q = q_ref[rows, columns]
        ga = ga_ref[rows, columns]
        k = keys[near]
        v = values[near]
        probs = softmax(q, k, mask_ref[3 * b * BLOCK : 3 * (b + 1) * BLOCK, :], scale)
        probs_bf = probs.astype(jnp.bfloat16)
        if att_ref is not None:
            att_ref[columns, rows] = left_dot(v, probs_bf).astype(jnp.bfloat16)
        grad_probs = right_dot(v, ga)
        inner = jnp.sum(probs * grad_probs, axis=0, keepdims=True)
        scores_bf = (probs * (grad_probs - inner) * scale).astype(jnp.bfloat16)
        gq_ref[rows, columns] = left_dot(scores_bf, k).astype(jnp.bfloat16)
        key_terms = plain_dot(scores_bf, q)
        value_terms = plain_dot(probs_bf, ga)
        for j in range(3):
            part = slice(j * size, (j + 1) * size)
            for sums, terms in ((key_sums, key_terms), (value_sums, value_terms)):
                old = sums[b + j]
                sums[b + j] = terms[part] if old is None else old + terms[part]
    for sums, own, halo in ((key_sums, kto_ref, kth_ref), (value_sums, vto_ref, vth_ref)):
        halo[:size, columns] = sums[0].astype(jnp.bfloat16)
        halo[size:, columns] = sums[blocks + 1].astype(jnp.bfloat16)
        for b in range(blocks):
            own[b * size : (b + 1) * size, columns] = sums[b + 1].astype(jnp.bfloat16)


def turn(from_ref, to_ref):
    rows = from_ref.shape[0]
    down = lax.broadcasted_iota(jnp.int32, (rows, rows), 0)
    across = lax.broadcasted_iota(jnp.int32, (rows, rows), 1)
    identity = jnp.where(down == across, 1.0, 0.0).astype(jnp.bfloat16)
    to_ref[...] = left_dot(from_ref[...], identity).astype(jnp.bfloat16)


def heads_of(q, scale):
    dim = round(1.0 / scale**2)
    return [slice(first, first + dim) for first in range(0, q.shape[1], dim)]


def forward_kernel(scale, q, ko, vo, kh, vh, mask, no, nh, att, not_, nht):
    for columns in heads_of(q, scale):
        head_forward(scale, columns, q, ko, vo, kh, vh, mask, att)
    turn(no, not_)
    turn(nh, nht)


def both_kernel(
    scale, q, ko, vo, kh, vh, mask, no, nh, ga, att, not_, nht, gq, kto, vto, kth, vth
):
    for columns in heads_of(q, scale):
        head_backward(scale, columns, q, ko, vo, kh, vh, ga, mask, gq, kto, vto, kth, vth, att)
    turn(no, not_)
    turn(nh, nht)


def attention(q, ko, vo, kh, vh, mask, no, nh, ga=None):
    rows, features = q.shape
    dim = features // HEADS
    halo = kh.shape[0]
    flat = lambda n: pl.BlockSpec((n, GROUP * dim), lambda h: (0, h))
    tall = lambda n: pl.BlockSpec((GROUP * dim, n), lambda h: (h, 0))
    shape = lambda n: jax.ShapeDtypeStruct((n, features), jnp.bfloat16)
    tall_shape = lambda n: jax.ShapeDtypeStruct((features, n), jnp.bfloat16)
    in_specs = [flat(rows), flat(rows), flat(rows), flat(halo), flat(halo)]
    in_specs += [pl.BlockSpec(mask.shape, lambda h: (0, 0)), flat(rows), flat(halo)]
    out_specs = [tall(rows), tall(rows), tall(halo)]
    out_shape = [tall_shape(rows), tall_shape(rows), tall_shape(halo)]
    operands = [q, ko, vo, kh, vh, mask, no, nh]
    if ga is not None:
        in_specs.append(flat(rows))
        operands.append(ga)
        out_specs += [flat(rows), flat(rows), flat(rows), flat(halo), flat(halo)]
        out_shape += [shape(rows), shape(rows), shape(rows), shape(halo), shape(halo)]
    return pl.pallas_call(
        functools.partial(
            forward_kernel if ga is None else both_kernel, 1.0 / math.sqrt(dim)
        ),
        grid=(HEADS // GROUP,),
        in_specs=in_specs,
        out_specs=out_specs,
        out_shape=out_shape,
        cost_estimate=pl.CostEstimate(
            flops=(4 if ga is None else 12) * rows * 3 * BLOCK * features,
            bytes_accessed=24 * rows * features,
            transcendentals=rows * 3 * BLOCK * HEADS,
        ),
        name="attention_forward" if ga is None else "attention_both_ways",
    )(*operands)


def bit_orders(bits):
    swapped = [1, 0] + list(range(2, bits))
    late = list(range(2, bits)) + [0, 1]
    return (list(range(bits)), swapped, late)


QUARTERS = 4
PORTIONS = ((3, 0, 0), (3, 1, 1), (3, 2, 2), (3, 3, 2)) + tuple(
    (projection, quarter, quarter % 2) for projection in range(3) for quarter in range(QUARTERS)
)
EARLY = 4
LAG = 2
AHEAD = 3


def last_kernel(
    count, n0, nh0, n1, nh1, att0, att1, gq0, ko0, vo0, kh0, vh0, up0, up1,
    q1, key1, value1, key_halo1, value_halo1, mask, x1, wq, wk, wv, wo, grad_x0,
    out_ref, grad_x_ref,
    nlhs, alhs, keep, send, recv, ga1, gq1, ko1, vo1, kh1, vh1, term, term_in,
    send_sem, recv_sem, term_send, term_recv,
):
    me = lax.axis_index("mesh")
    bits = count.bit_length() - 1
    orders = bit_orders(bits)
    features = n0.shape[0]
    rows_here = x1.shape[0]
    chunk = features // count
    width = features // QUARTERS
    scale = 1.0 / math.sqrt(features // HEADS)
    after = lax.rem(me + 1, count)
    before = lax.rem(me + count - 1, count)

    def bit_of(b):
        return lax.rem(me // (1 << b), 2)

    def partner(b):
        return me + (1 - 2 * bit_of(b)) * (1 << b)

    barrier = pltpu.get_barrier_semaphore()
    for other in [before, after] + [partner(b) for b in range(bits)]:
        pl.semaphore_signal(barrier, inc=1, device_id={"mesh": other}, device_id_type=MESH)

    def chunk_rows(order, place):
        index = 0
        for k, b in enumerate(order):
            here = bit_of(b)
            flip = (place >> (bits - 1 - k)) & 1
            index = index + (1 - here if flip else here) * (1 << b)
        return pl.ds(pl.multiple_of(index * chunk, chunk), chunk)

    def arrange(to_ref, slot, order, parts):
        for place in range(count):
            rows = chunk_rows(order, place)
            first = 0
            for part in parts:
                last = first + part.shape[1]
                to_ref[slot, place * chunk : (place + 1) * chunk, first:last] = part[rows, :]
                first = last

    rights = ((gq0, gq1), (ko0, ko1, kh0, kh1), (vo0, vo1, vh0, vh1), (up0, up1))

    def columns_of(portion):
        return slice(portion[1] * width, (portion[1] + 1) * width)

    def product(portion, rows):
        projection, _, order = portion
        right = jnp.concatenate([r[:, columns_of(portion)] for r in rights[projection]], axis=0)
        left = alhs if projection == 3 else nlhs
        return plain_dot(left[order, rows, : right.shape[0]], right)

    starts = []
    first = 0
    for k in range(bits):
        starts.append(first)
        first += features >> (k + 1)

    def copy_of(p, k):
        rows = pl.ds(starts[k], features >> (k + 1))
        return pltpu.make_async_remote_copy(
            src_ref=send.at[p, rows],
            dst_ref=recv.at[p, rows],
            send_sem=send_sem.at[p, k],
            recv_sem=recv_sem.at[p, k],
            device_id={"mesh": partner(orders[PORTIONS[p][2]][k])},
            device_id_type=MESH,
        )

    def term_copy(side):
        return pltpu.make_async_remote_copy(
            src_ref=term.at[pl.ds(side * BLOCK, BLOCK)],
            dst_ref=term_in.at[pl.ds((1 - side) * BLOCK, BLOCK)],
            send_sem=term_send.at[side],
            recv_sem=term_recv.at[1 - side],
            device_id={"mesh": after if side else before},
            device_id_type=MESH,
        )

    def arrived(side):
        return term_copy(1 - side)

    middle = features // 2

    def begin(p):
        send[p, :middle] = product(PORTIONS[p], slice(middle, features)).astype(jnp.bfloat16)
        copy_of(p, 0).start()

    for slot, order in enumerate(orders):
        arrange(alhs, slot, order, (att0, att1))
    pl.semaphore_wait(barrier, bits + 2)
    for p in range(EARLY):
        begin(p)

    ga1[...] = right_dot(up1[...], wo[...]).astype(jnp.bfloat16)
    dim = features // HEADS

    def heads(first, last):
        @pl.loop(first, last)
        def _(pair):
            for h in range(GROUP):
                columns = pl.ds(pl.multiple_of((pair * GROUP + h) * dim, dim), dim)
                head_backward(
                    scale, columns, q1, key1, value1, key_halo1, value_halo1, ga1, mask,
                    gq1, ko1, vo1, kh1, vh1,
                )

    def advance(p, k):
        portion = PORTIONS[p]
        size = features >> (k + 1)
        if k == 0:
            keep[p] = product(portion, slice(0, middle))
        copy_of(p, k).wait_recv()
        if k + 1 < bits:
            left = size // 2
            send[p, starts[k + 1] : starts[k + 1] + left] = (
                keep[p, left:size]
                + recv[p, starts[k] + left : starts[k] + size].astype(jnp.float32)
            ).astype(jnp.bfloat16)
            copy_of(p, k + 1).start()
            keep[p, :left] += recv[p, starts[k] : starts[k] + left].astype(jnp.float32)
        else:
            out_ref[:, portion[0], columns_of(portion)] = keep[p, :size] + recv[
                p, starts[k] : starts[k] + size
            ].astype(jnp.float32)

    groups = HEADS // GROUP
    done = 0
    for k, last in enumerate((groups // 2, 3 * groups // 4, groups)):
        heads(done, last)
        done = last
        for p in range(EARLY):
            advance(p, k)

    term[...] = (right_dot(kh1[...], wk[...]) + right_dot(vh1[...], wv[...])).astype(jnp.bfloat16)
    for side in (0, 1):
        term_copy(side).start()
    for slot in (0, 1):
        arrange(nlhs, slot, orders[slot], (n0, n1, nh0, nh1))
    for p in range(EARLY, EARLY + AHEAD):
        begin(p)
    def finish_input():
        x_float = x1[...].astype(jnp.float32)
        inv_rms = lax.rsqrt(jnp.mean(x_float * x_float, axis=-1, keepdims=True) + EPSILON)
        normed = x_float * inv_rms
        grad = right_dot(gq1[...], wq[...])
        grad = grad + right_dot(ko1[...], wk[...]) + right_dot(vo1[...], wv[...])
        for side in (0, 1):
            arrived(side).wait_recv()
        pieces = [term_in[:BLOCK].astype(jnp.float32)]
        if rows_here > 2 * BLOCK:
            pieces.append(jnp.zeros((rows_here - 2 * BLOCK, features), jnp.float32))
        pieces.append(term_in[BLOCK:].astype(jnp.float32))
        grad = grad + jnp.concatenate(pieces, axis=0)
        grad = inv_rms * (grad - normed * jnp.mean(grad * normed, axis=-1, keepdims=True))
        grad_x_ref[0] = grad_x0[...]
        grad_x_ref[1] = (up1[...].astype(jnp.float32) + grad).astype(jnp.bfloat16)

    for p in range(EARLY):
        for k in range(3, bits):
            advance(p, k)
    rest = range(EARLY, len(PORTIONS))
    for stage in range(len(rest) + LAG * (bits - 1)):
        if stage + AHEAD < len(rest):
            begin(rest[stage + AHEAD])
        for k in reversed(range(bits)):
            place = stage - LAG * k
            if 0 <= place < len(rest):
                advance(rest[place], k)
        if stage == LAG:
            finish_input()
    for k in range(bits):
        for p in range(len(PORTIONS)):
            copy_of(p, k).wait_send()
    for side in (0, 1):
        term_copy(side).wait_send()


def last_tick(*operands):
    count = lax.axis_size("mesh")
    bits = count.bit_length() - 1
    features, rows = operands[0].shape
    halo = operands[1].shape[1]
    chunk = features // count
    portions = len(PORTIONS)
    moved = features - chunk
    width = features // QUARTERS
    half = lambda *shape: pltpu.VMEM(shape, jnp.bfloat16)
    return pl.pallas_call(
        functools.partial(last_kernel, count),
        out_shape=[
            jax.ShapeDtypeStruct((chunk, 4, features), jnp.float32),
            jax.ShapeDtypeStruct((2, rows, features), jnp.bfloat16),
        ],
        in_specs=[pl.BlockSpec(memory_space=pltpu.VMEM)] * len(operands),
        out_specs=[pl.BlockSpec(memory_space=pltpu.VMEM)] * 2,
        scratch_shapes=[
            half(2, features, 2 * (rows + halo)),
            half(3, features, 2 * rows),
            pltpu.VMEM((portions, features // 2, width), jnp.float32),
            half(portions, moved, width),
            half(portions, moved, width),
            half(rows, features),
            half(rows, features),
            half(rows, features),
            half(rows, features),
            half(halo, features),
            half(halo, features),
            half(halo, features),
            half(halo, features),
            pltpu.SemaphoreType.DMA((portions, bits)),
            pltpu.SemaphoreType.DMA((portions, bits)),
            pltpu.SemaphoreType.DMA((2,)),
            pltpu.SemaphoreType.DMA((2,)),
        ],
        compiler_params=pltpu.CompilerParams(
            collective_id=0, has_side_effects=True, vmem_limit_bytes=60 * 2**20
        ),
        cost_estimate=pl.CostEstimate(
            flops=4 * features * features * (4 * rows + 2 * halo),
            bytes_accessed=200 * 2**20,
            transcendentals=0,
        ),
        name="last_tick",
    )(*operands)


def per_device(
    saved_inputs, w_query, w_key, w_value, w_out, pending, top_grads, key_blocks, counts, plan
):
    sections = lax.axis_size("section")
    section_here = lax.axis_index("section")
    part_here = lax.axis_index("mesh")
    rows_here = pending.shape[1]
    features = pending.shape[2]
    blocks_here = rows_here // BLOCK
    query_weight = w_query[0]
    key_weight = w_key[0]
    value_weight = w_value[0]
    out_weight = w_out[0]

    def norm(x):
        x_float = x.astype(jnp.float32)
        inv_rms = lax.rsqrt(jnp.mean(x_float * x_float, axis=-1, keepdims=True) + EPSILON)
        normed_float = x_float * inv_rms
        return inv_rms, normed_float, normed_float.astype(jnp.bfloat16)

    def project(normed, weight):
        return plain_dot(normed, weight).astype(jnp.bfloat16)

    members = lax.dynamic_index_in_dim(plan, section_here, 1, keepdims=False)
    inputs = [
        lax.dynamic_index_in_dim(saved_inputs[0], members[t], 0, keepdims=False) for t in (0, 1)
    ]

    def halo_of(x):
        return jnp.concatenate(
            [
                from_behind(x[rows_here - BLOCK :], "mesh", 1),
                from_behind(x[:BLOCK], "mesh", -1),
            ],
            axis=0,
        )

    halos = [halo_of(x) for x in inputs]

    positions = jnp.arange(BLOCK)
    block_ids = jnp.arange(counts.shape[0])
    global_ids = part_here * blocks_here + jnp.arange(blocks_here)
    near_ids = jnp.stack([key_blocks[:, 1], global_ids, key_blocks[:, 0]], axis=1)
    near_counts = jnp.sum(
        jnp.where(block_ids[None, None, :] == near_ids[:, :, None], counts[None, None, :], 0),
        axis=2,
    )
    mask = jnp.where(positions[None, None, :] < near_counts[:, :, None], 0.0, -jnp.inf)
    mask = jnp.broadcast_to(
        mask.reshape(blocks_here * 3 * BLOCK, 1).astype(jnp.float32), (blocks_here * 3 * BLOCK, BLOCK)
    )

    def ready(t):
        normed = norm(inputs[t])[2]
        own = [project(normed, w) for w in (query_weight, key_weight, value_weight)]
        normed_halo = norm(halos[t])[2]
        near = [project(normed_halo, w) for w in (key_weight, value_weight)]
        return own + near + [mask, normed, normed_halo]

    upstream = pending[0]
    first = ready(0)
    grad_attended = right_dot(upstream, out_weight).astype(jnp.bfloat16)
    att0, n0, nh0, gq, ko, vo, kh, vh = attention(*first, grad_attended)
    halo_term = (right_dot(kh, key_weight) + right_dot(vh, value_weight)).astype(jnp.bfloat16)
    halo_term, halos[1] = lax.optimization_barrier((halo_term, halos[1]))
    from_after = from_behind(halo_term[:BLOCK], "mesh", -1)
    from_before = from_behind(halo_term[BLOCK:], "mesh", 1)
    second = ready(1)
    att1, n1, nh1 = attention(*second)
    from_after, from_before, att1 = lax.optimization_barrier((from_after, from_before, att1))
    grad_normed = (
        right_dot(gq, query_weight) + right_dot(ko, key_weight) + right_dot(vo, value_weight)
    )
    middle = jnp.zeros((rows_here - 2 * BLOCK, features), jnp.bfloat16)
    grad_normed = grad_normed + jnp.concatenate([from_before, middle, from_after], axis=0).astype(
        jnp.float32
    )
    inv_rms, normed_float, _ = norm(inputs[0])
    grad_input = inv_rms * (
        grad_normed - normed_float * jnp.mean(grad_normed * normed_float, axis=-1, keepdims=True)
    )
    grad_x = (upstream.astype(jnp.float32) + grad_input).astype(jnp.bfloat16)
    passed = shifted(grad_x, "section", -1)
    later = jnp.where(section_here == sections - 1, top_grads[0], passed)
    layer_total, input_grads = last_tick(
        n0, nh0, n1, nh1, att0, att1, gq, ko, vo, kh, vh, upstream, later,
        *second[:6], inputs[1], query_weight, key_weight, value_weight, out_weight, grad_x,
    )
    return (layer_total[None], input_grads[:, None])


def solution(mesh):
    in_specs = (
        P("section", None, "mesh", None),
        P("section", None, None),
        P("section", None, None),
        P("section", None, None),
        P("section", None, None),
        P("section", "mesh", None),
        P(None, "mesh", None),
        P("mesh", None),
        P(),
        P(),
    )
    out_specs = (P("section", "mesh", None, None), P(None, "section", "mesh", None))
    return jax.shard_map(
        per_device, mesh=mesh, in_specs=in_specs, out_specs=out_specs, check_vma=False
    )
```
